768 devices in a mesh: row: 16 (over y, z_hi), col: 8 (over x, core), layer: 6 (over z_lo).
Axes of the slice: x: 4, y: 8, z: 12 (z_hi: 2, z_lo: 6; z = z_hi * 6 + z_lo), core: 2. Of those that a mesh axis runs over, the one named last changes fastest.
Arguments:
- left_tiles: bfloat16 [6, 16, 16, 6, 256, 256], P('layer', 'row', 'col'), may hold values from -6 to 6
- left_place: int32 [6, 16, 16, 6], P('layer', 'row', 'col'), may hold values from -1 to 23, as said below
- right_tiles: bfloat16 [6, 16, 16, 2, 256, 256], P('layer', 'row', 'col'), may hold values from -0.1875 to 0.1875
- right_place: int32 [6, 16, 16, 2], P('layer', 'row', 'col'), may hold values from -1 to 7, as said below
Outputs:
- product: bfloat16 [12288, 4096], P(('row', 'layer'), 'col')
The draws below stay inside these ranges and needn't reach their ends.
Inputs may be any that keep to these rules, and one draw needn't show every extreme that they name: `left_place`: in each block the occupied slots come first, name distinct tile positions, and at least one slot is occupied; -1 marks an empty slot. `right_place`: in each block the occupied slots come first, name distinct tile positions, and at least one slot is occupied; -1 marks an empty slot.
All inputs are finite; a program needn't handle non-finite values.
Results may differ from the reference program's by a relative error of at most 0.015.
Values may be sent and summed in bfloat16 or wider, within the bound.
No kernel may reach another device: no remote copies, remote signals or barrier semaphores. Data moves between devices by JAX's collectives and lax.ppermute only.
A program may use at most 32 MiB of HBM per device.

```python
import jax
import jax.numpy as jnp
from jax import lax

TS = 256
KT = 8
RT = 3
CT = 1
SA = 6
SB = 2
STEPS = 4
GRID = 16
N_LAYER = 6


def slot_lists(key, capacity, positions):
    block_count = N_LAYER * GRID * GRID
    score_key, count_key = jax.random.split(key)
    scores = jax.random.randint(score_key, (block_count, positions), 0, 1 << 20) * positions + jnp.arange(positions, dtype=jnp.int32)[None, :]
    chosen = jnp.argsort(scores, axis=1)[:, :capacity].astype(jnp.int32)
    chosen = chosen.at[0].set(positions - 1 - jnp.arange(capacity, dtype=jnp.int32))
    counts = jax.random.randint(count_key, (block_count,), 1, capacity + 1)
    counts = counts.at[0].set(capacity).at[1].set(1)
    slot_ids = jnp.arange(capacity, dtype=jnp.int32)
    places = jnp.where(slot_ids[None, :] < counts[:, None], chosen, -1)
    return places.reshape(N_LAYER, GRID, GRID, capacity).astype(jnp.int32)


def draw_left_place(key, part):
    key = jax.random.fold_in(key, 11)
    return slot_lists(key, SA, RT * KT)


def draw_right_place(key, part):
    key = jax.random.fold_in(key, 23)
    return slot_lists(key, SB, KT * CT)


def levels(own_key, extent, cuts, least, largest):
    factor_of = 1.0
    for axis_at, shards_of in cuts:
        heights = jax.random.uniform(jax.random.fold_in(jax.random.fold_in(own_key, 6), axis_at), (shards_of,), jnp.float32, least / len(cuts), largest / len(cuts))
        factor_of = factor_of * jnp.repeat(jnp.exp(heights), extent[axis_at] // shards_of).reshape((-1,) + (1,) * (len(extent) - 1 - axis_at))
    return factor_of


def scatter_about(stream_key, dims, width, reach, cuts=(), kind=jnp.bfloat16):
    entries = jax.random.normal(stream_key, dims, jnp.float32) * width
    if len(cuts) > 0:
        entries = levels(stream_key, dims, cuts, -0.22, 0.18) * entries
    return jnp.clip(entries, min=-reach, max=reach).astype(kind)


def setup_inputs(seed: int = 0) -> dict:
    streams_of = jax.random.split(jax.random.key(seed), 5)
    left_tiles = scatter_about(streams_of[0], (N_LAYER, GRID, GRID, SA, TS, TS), 1.0, 6.0, ((0, 6), (1, 16), (2, 8)))
    left_place = draw_left_place(jax.random.fold_in(streams_of[4], 71), 0)
    right_tiles = scatter_about(streams_of[2], (N_LAYER, GRID, GRID, SB, TS, TS), (4 * TS) ** -0.5, 0.1875, ((0, 6), (1, 16), (2, 8)))
    right_place = draw_right_place(jax.random.fold_in(streams_of[4], 71), 0)
    return {"left_tiles": left_tiles, "left_place": left_place, "right_tiles": right_tiles, "right_place": right_place}


def block_product(left_block, left_slots, right_block, right_slots):
    inner_left = left_slots % KT
    row_left = jnp.where(left_slots >= 0, left_slots // KT, -1)
    inner_right = jnp.where(right_slots >= 0, right_slots // CT, -1)
    column_right = right_slots % CT
    columns = jnp.arange(CT, dtype=jnp.int32)
    select = ((inner_right[None, :, None] == inner_left[:, None, None]) & (column_right[None, :, None] == columns[None, None, :])).astype(jnp.float32)
    right_strip = jnp.einsum("abc,bxy->axcy", select, right_block.astype(jnp.float32)).reshape(left_block.shape[0], TS, CT * TS)
    partial_rows = jnp.einsum("axy,ayz->axz", left_block.astype(jnp.float32), right_strip)
    rowhot = (row_left[:, None] == jnp.arange(RT, dtype=jnp.int32)[None, :]).astype(jnp.float32)
    return jnp.einsum("ar,axz->rxz", rowhot, partial_rows).reshape(RT * TS, CT * TS)


def reference(left_tiles, left_place, right_tiles, right_place):
    grid_size = left_tiles.shape[1]
    columns = jnp.arange(grid_size, dtype=jnp.int32)

    def one_row(row_index):
        running = jnp.zeros((grid_size, RT * TS, CT * TS), jnp.float32)
        for slab_index in range(N_LAYER):
            partial_sum = jnp.zeros((grid_size, RT * TS, CT * TS), jnp.float32)
            for advance in range(STEPS):
                source = (columns + advance) % grid_size
                left_blocks = left_tiles[slab_index, row_index][source]
                left_slots = left_place[slab_index, row_index][source]
                right_row = ((row_index + advance) % grid_size).astype(jnp.int32)
                right_blocks = right_tiles[slab_index, right_row]
                right_slots = right_place[slab_index, right_row]
                partial_sum = partial_sum + jax.vmap(block_product)(left_blocks, left_slots, right_blocks, right_slots)
            rounded = lax.optimization_barrier(partial_sum.astype(jnp.bfloat16))
            running = running + rounded.astype(jnp.float32)
        return running.astype(jnp.bfloat16)

    rows_out = lax.map(one_row, jnp.arange(grid_size, dtype=jnp.int32))
    return rows_out.transpose(0, 2, 1, 3).reshape(grid_size * RT * TS, grid_size * CT * TS)
```

```python
import functools

import jax
import jax.numpy as jnp
from jax import lax
from jax.experimental import pallas as pl
from jax.experimental.pallas import tpu as pltpu
from jax.sharding import PartitionSpec as P

TS = 256
KT = 8
RT = 3
SA = 6
SB = 2
STEPS = 4
GRID = 16
N_LAYER = 6
HELD = 2


def shifted(block, axis, distance):
    size = lax.axis_size(axis)
    return lax.ppermute(block, axis, [((i - distance) % size, i) for i in range(size)])


def add_term(total, at_ref, left_table, right_table, left_ref, right_ref, column, step):
    left_at = lax.rem(at_ref[0] + (column + step), GRID)
    right_at = lax.rem(at_ref[1] + step, GRID) * HELD + column
    first = right_table[right_at * SB]
    second = right_table[right_at * SB + 1]

    def slot(q, carry):
        place = left_table[left_at * SA + q]
        inner = lax.rem(place, KT)
        used = place >= 0
        hits_first = used & (first == inner)
        hits_second = used & (second == inner)

        @pl.when(hits_first | hits_second)
        def _():
            rows = pl.ds(pl.multiple_of((place // KT) * TS, TS), TS)
            tile = jnp.where(hits_first, 0, 1)
            total[rows, :] += jnp.dot(left_ref[q], right_ref[tile], preferred_element_type=jnp.float32)

        return carry

    lax.fori_loop(0, SA, slot, 0)


def early_kernel(at_ref, left_table, right_table, *refs, terms):
    operands, total = refs[:-1], refs[-1]
    total[...] = jnp.zeros_like(total)
    for n, (column, step) in enumerate(terms):
        add_term(total.at[column], at_ref, left_table, right_table, operands[2 * n], operands[2 * n + 1], column, step)


def late_kernel(at_ref, left_table, right_table, start_ref, *refs, terms):
    operands, out_ref, total = refs[:-2], refs[-2], refs[-1]
    total[...] = start_ref[...]
    for n, (column, step) in enumerate(terms):
        add_term(total, at_ref, left_table, right_table, operands[2 * n], operands[2 * n + 1], column, step)
    out_ref[...] = total[...].astype(out_ref.dtype)


SMEM = pl.BlockSpec(memory_space=pltpu.SMEM)
VMEM = pl.BlockSpec(memory_space=pltpu.VMEM)
PARAMS = pltpu.CompilerParams(vmem_limit_bytes=32 * 1024 * 1024)


def early(tables, terms, operands):
    return pl.pallas_call(
        functools.partial(early_kernel, terms=terms),
        out_shape=jax.ShapeDtypeStruct((HELD, RT * TS, TS), jnp.float32),
        in_specs=[SMEM] * 3 + [VMEM] * len(operands),
        out_specs=VMEM,
        compiler_params=PARAMS,
        cost_estimate=pl.CostEstimate(flops=len(terms) * 3 * 2 * TS**3, bytes_accessed=6 << 20, transcendentals=0),
    )(*tables, *operands)


def late(tables, terms, start, operands):
    return pl.pallas_call(
        functools.partial(late_kernel, terms=terms),
        out_shape=jax.ShapeDtypeStruct((RT * TS, TS), jnp.bfloat16),
        in_specs=[SMEM] * 3 + [VMEM] * (1 + len(operands)),
        out_specs=VMEM,
        scratch_shapes=[pltpu.VMEM((RT * TS, TS), jnp.float32)],
        compiler_params=PARAMS,
        cost_estimate=pl.CostEstimate(flops=len(terms) * 3 * 2 * TS**3, bytes_accessed=4 << 20, transcendentals=0),
    )(*tables, start, *operands)


def body(left_tiles, left_place, right_tiles, right_place):
    left = left_tiles[0, 0]
    right = right_tiles[0, 0]
    with jax.named_scope("cross"):
        right_one = [shifted(right[j], "row", -1) for j in range(HELD)]
    with jax.named_scope("left"):
        left_next = shifted(left, "col", -1)
        left_last = shifted(left_next[0], "col", -1)
    with jax.named_scope("right_two"):
        right_two = shifted(right, "row", -2)
    with jax.named_scope("tables"):
        left_table = lax.all_gather(left_place[0, 0], "col", tiled=True).reshape(-1)
        right_table = lax.all_gather(right_place[0, 0], "row", tiled=True).reshape(-1)
    at = jnp.stack([lax.axis_index("col") * HELD, lax.axis_index("row")]).astype(jnp.int32)
    tables = (at, left_table, right_table)
    lefts = [left[0], left[1], left_next[0], left_next[1], left_last]
    first = [(j, s) for j in range(HELD) for s in (0, 2)]
    totals = early(
        tables, first, [x for j, s in first for x in (lefts[j + s], (right if s == 0 else right_two)[j])]
    )
    parts = []
    for j in range(HELD):
        right_three = shifted(right_one[j], "row", -2)
        partial = late(
            tables, [(j, 1), (j, 3)], totals[j], [lefts[j + 1], right_one[j], lefts[j + 3], right_three]
        )
        shares = lax.all_to_all(partial.reshape(N_LAYER, -1, TS), "layer", 0, 0, tiled=True)
        parts.append(jnp.sum(shares.astype(jnp.float32), axis=0).astype(jnp.bfloat16))
    return jnp.concatenate(parts, axis=1)


def solution(mesh):
    return jax.shard_map(
        body,
        mesh=mesh,
        in_specs=(
            P("layer", "row", "col", None, None, None),
            P("layer", "row", "col", None),
            P("layer", "row", "col", None, None, None),
            P("layer", "row", "col", None),
        ),
        out_specs=P(("row", "layer"), "col"),
        check_vma=False,
    )
```

```python
import functools

import jax
import jax.numpy as jnp
from jax import lax
from jax.experimental import pallas as pl
from jax.experimental.pallas import tpu as pltpu
from jax.sharding import PartitionSpec as P

TS = 256
KT = 8
RT = 3
SA = 6
SB = 2
TRIO = 3
SHARE = 128
HELD = 2
NOTE = 16
PIECE = SB * TS + NOTE
BLOCK = SA * TS + NOTE


def shifted(block, axis, distance):
    size = lax.axis_size(axis)
    return lax.ppermute(block, axis, [((i - distance) % size, i) for i in range(size)])


def add_term(total, place_ref, left_ref, right_ref):
    first, second = noted(right_ref, SB)
    for q, place in enumerate(noted(left_ref, SA)):
        place_ref[q] = place

    def slot(q, carry):
        place = place_ref[q]
        inner = lax.rem(place, KT)
        used = place >= 0
        hits_first = used & (first == inner)
        hits_second = used & (second == inner)

        @pl.when(hits_first | hits_second)
        def _():
            left_rows = pl.ds(pl.multiple_of(q * TS, TS), TS)
            right_rows = pl.ds(pl.multiple_of(jnp.where(hits_first, 0, TS), TS), TS)
            rows = pl.ds(pl.multiple_of((place // KT) * TS, TS), TS)
            total[rows, :] += jnp.dot(
                left_ref[left_rows, :], right_ref[right_rows, :], preferred_element_type=jnp.float32
            )

        return carry

    lax.fori_loop(0, SA, slot, 0)


def noted(packed_ref, slots):
    note = packed_ref[slots * TS : slots * TS + NOTE, :128].astype(jnp.float32).astype(jnp.int32)
    return [note[0, p] for p in range(slots)]


def write_note(packed_ref, place_ref, column, slots):
    shape = (NOTE, packed_ref.shape[1])
    lane = lax.broadcasted_iota(jnp.int32, shape, 1)
    note = jnp.full(shape, -1, jnp.int32)
    for p in range(slots):
        note = jnp.where(lane == p, place_ref[column, p], note)
    packed_ref[slots * TS :, :] = note.astype(jnp.float32).astype(jnp.bfloat16)


def pack_right_kernel(place_ref, right_ref, *pieces):
    for column, piece in enumerate(pieces):
        for p in range(SB):
            piece[p * TS : (p + 1) * TS, :] = right_ref[column, p]
        write_note(piece, place_ref, column, SB)


def pack_left_kernel(place_ref, left_ref, right_zero, right_one, lefts, left_zero, rights):
    for column in range(HELD):
        targets = [lefts.at[column * BLOCK : (column + 1) * BLOCK]] + [left_zero] * (column == 0)
        for target in targets:
            for q in range(SA):
                target[q * TS : (q + 1) * TS, :] = left_ref[column, q]
            write_note(target, place_ref, column, SA)
    rights[:PIECE, :] = right_zero[...]
    rights[PIECE:, :] = right_one[...]


def early_kernel(own, after, rights, twos, *refs):
    totals, place_ref = refs[:-1], refs[-1]
    for column, total in enumerate(totals):
        left = pl.ds(column * BLOCK, BLOCK)
        right = pl.ds(column * PIECE, PIECE)
        total[...] = jnp.zeros_like(total)
        add_term(total, place_ref, own.at[left], rights.at[right])
        add_term(total, place_ref, after.at[left], twos.at[right])


def late_kernel(layer, start_ref, left_one, left_three, right_one, right_three, *refs, blocks):
    share_refs, total, place_ref = refs[:-2], refs[-2], refs[-1]
    total[...] = start_ref[...]
    for left, block, right in ((left_one, blocks[0], right_one), (left_three, blocks[1], right_three)):
        add_term(total, place_ref, left.at[pl.ds(block * BLOCK, BLOCK)], right)
    half = layer[0] // TRIO
    for turn, share in enumerate(share_refs):
        spot = lax.rem(layer[0] + turn, TRIO)
        for n, side in enumerate((half, 1 - half)):
            rows = pl.ds(pl.multiple_of((side * TRIO + spot) * SHARE, SHARE), SHARE)
            share[n * SHARE : (n + 1) * SHARE, :] = total[rows, :].astype(share.dtype)


def gather_kernel(own, one, two, near, far):
    added = own[...].astype(jnp.float32) + one[...].astype(jnp.float32) + two[...].astype(jnp.float32)
    near[...] = added[:SHARE]
    far[...] = added[SHARE:].astype(far.dtype)


def final_kernel(*refs):
    out_ref = refs[-1]
    for n in range(HELD):
        added = refs[2 * n][...] + refs[2 * n + 1][...].astype(jnp.float32)
        out_ref[:, n * TS : (n + 1) * TS] = added.astype(out_ref.dtype)


AHEAD = 10**12
SMEM = pl.BlockSpec(memory_space=pltpu.SMEM)
VMEM = pl.BlockSpec(memory_space=pltpu.VMEM)
PARAMS = pltpu.CompilerParams(vmem_limit_bytes=32 * 1024 * 1024)


def call(kernel, out_shape, in_specs, operands, scratch=(), cost=0):
    return pl.pallas_call(
        kernel,
        out_shape=out_shape,
        in_specs=in_specs,
        out_specs=jax.tree.map(lambda _: VMEM, out_shape),
        scratch_shapes=scratch,
        compiler_params=PARAMS,
        cost_estimate=pl.CostEstimate(flops=cost, bytes_accessed=0, transcendentals=0),
    )(*operands)


def array(rows, columns, dtype=jnp.bfloat16):
    return jax.ShapeDtypeStruct((rows, columns), dtype)


def body(left_tiles, left_place, right_tiles, right_place):
    layer = lax.axis_index("layer").astype(jnp.int32).reshape(1)
    places = pltpu.SMEM((SA,), jnp.int32)
    pieces = call(
        pack_right_kernel,
        [array(PIECE, TS)] * HELD,
        [SMEM, VMEM],
        (right_place[0, 0], right_tiles[0, 0]),
    )
    right_one = [shifted(piece, "row", -1) for piece in pieces]
    lefts, left_zero, rights = call(
        pack_left_kernel,
        [array(HELD * BLOCK, TS), array(BLOCK, TS), array(HELD * PIECE, TS)],
        [SMEM] + [VMEM] * 3,
        (left_place[0, 0], left_tiles[0, 0], *pieces),
    )
    right_two = shifted(rights, "row", -2)
    left_next = shifted(lefts, "col", -1)
    left_last = shifted(left_zero, "col", -2)
    totals = call(
        early_kernel,
        [array(RT * TS, TS, jnp.float32)] * HELD,
        [VMEM] * 4,
        (lefts, left_next, rights, right_two),
        [places],
    )
    right_one[1], totals = lax.optimization_barrier((right_one[1], totals))
    right_three = [shifted(piece, "row", -2) for piece in right_one]
    held = [(lefts, 0), (lefts, 1), (left_next, 0), (left_next, 1), (left_last, 0)]
    trio = [[(p, p // TRIO * TRIO + (p + turn) % TRIO) for p in range(2 * TRIO)] for turn in range(TRIO)]
    across = [(p, (p + TRIO) % (2 * TRIO)) for p in range(2 * TRIO)]
    shares = []
    for j in range(HELD):
        if j:
            right_three[j], shares[j - 1] = lax.optimization_barrier((right_three[j], shares[j - 1]))
        (one, block_one), (three, block_three) = held[j + 1], held[j + 3]
        shares.append(
            call(
                functools.partial(late_kernel, blocks=(block_one, block_three)),
                [array(2 * SHARE, TS)] * TRIO,
                [SMEM] + [VMEM] * 5,
                (layer, totals[j], one, three, right_one[j], right_three[j]),
                [pltpu.VMEM((RT * TS, TS), jnp.float32), places],
            )
        )
    ends = []
    for j, (own_share, *others) in enumerate(shares):
        arrived = [lax.ppermute(share, "layer", trio[turn]) for turn, share in enumerate(others, 1)]
        if j:
            arrived, ends = lax.optimization_barrier((arrived, ends))
        near, far = call(
            gather_kernel,
            [array(SHARE, TS, jnp.float32), array(SHARE, TS)],
            [VMEM] * TRIO,
            (own_share, *arrived),
            cost=(1 - j) * AHEAD,
        )
        ends.append(near)
        shares[j] = far
    for j, far in enumerate(shares):
        ends.insert(2 * j + 1, lax.ppermute(far, "layer", across))
    return call(final_kernel, array(SHARE, HELD * TS), [VMEM] * len(ends), ends)


def solution(mesh):
    return jax.shard_map(
        body,
        mesh=mesh,
        in_specs=(
            P("layer", "row", "col", None, None, None),
            P("layer", "row", "col", None),
            P("layer", "row", "col", None, None, None),
            P("layer", "row", "col", None),
        ),
        out_specs=P(("row", "layer"), "col"),
        check_vma=False,
    )
```

```python
import functools

import jax
import jax.numpy as jnp
from jax import lax
from jax.experimental import pallas as pl
from jax.experimental.pallas import tpu as pltpu
from jax.sharding import PartitionSpec as P

TS = 256
KT = 8
RT = 3
SA = 6
SB = 2
TRIO = 3
SHARE = 128
HELD = 2
NOTE = 16
PIECE = SB * TS + NOTE
BLOCK = SA * TS + NOTE


def shifted(block, axis, distance):
    size = lax.axis_size(axis)
    return lax.ppermute(block, axis, [((i - distance) % size, i) for i in range(size)])


def add_term(total, place_ref, left_ref, right_ref):
    first, second = noted(right_ref, SB)
    for q, place in enumerate(noted(left_ref, SA)):
        place_ref[q] = place

    def slot(q, carry):
        place = place_ref[q]
        inner = lax.rem(place, KT)
        used = place >= 0
        hits_first = used & (first == inner)
        hits_second = used & (second == inner)

        @pl.when(hits_first | hits_second)
        def _():
            left_rows = pl.ds(pl.multiple_of(q * TS, TS), TS)
            right_rows = pl.ds(pl.multiple_of(jnp.where(hits_first, 0, TS), TS), TS)
            rows = pl.ds(pl.multiple_of((place // KT) * TS, TS), TS)
            total[rows, :] += jnp.dot(
                left_ref[left_rows, :], right_ref[right_rows, :], preferred_element_type=jnp.float32
            )

        return carry

    lax.fori_loop(0, SA, slot, 0)


def noted(packed_ref, slots):
    note = packed_ref[slots * TS : slots * TS + NOTE, :128].astype(jnp.float32).astype(jnp.int32)
    return [note[0, p] for p in range(slots)]


def write_note(packed_ref, place_ref, column, slots):
    shape = (NOTE, packed_ref.shape[1])
    lane = lax.broadcasted_iota(jnp.int32, shape, 1)
    note = jnp.full(shape, -1, jnp.int32)
    for p in range(slots):
        note = jnp.where(lane == p, place_ref[column, p], note)
    packed_ref[slots * TS :, :] = note.astype(jnp.float32).astype(jnp.bfloat16)


def pack_right_kernel(place_ref, right_ref, rights):
    for column in range(HELD):
        piece = rights.at[column * PIECE : (column + 1) * PIECE]
        for p in range(SB):
            piece[p * TS : (p + 1) * TS, :] = right_ref[column, p]
        write_note(piece, place_ref, column, SB)


def pack_left_kernel(place_ref, left_ref, lefts, left_zero):
    for column in range(HELD):
        targets = [lefts.at[column * BLOCK : (column + 1) * BLOCK]] + [left_zero] * (column == 0)
        for target in targets:
            for q in range(SA):
                target[q * TS : (q + 1) * TS, :] = left_ref[column, q]
            write_note(target, place_ref, column, SA)


def part(ref, column, rows):
    return ref.at[column * rows : (column + 1) * rows]


def local_kernel(lefts, rights, *refs):
    totals, place_ref = refs[:-1], refs[-1]
    for column, total in enumerate(totals):
        total[...] = jnp.zeros_like(total)
        add_term(total, place_ref, part(lefts, column, BLOCK), part(rights, column, PIECE))


def early_kernel(lefts, left_next, right_one, right_two, *refs):
    starts, totals, place_ref = refs[:HELD], refs[HELD:-1], refs[-1]
    for column, (start, total) in enumerate(zip(starts, totals)):
        total[...] = start[...]
        after = part(left_next, 0, BLOCK) if column else part(lefts, 1, BLOCK)
        add_term(total, place_ref, after, part(right_one, column, PIECE))
        add_term(total, place_ref, part(left_next, column, BLOCK), part(right_two, column, PIECE))


def late_kernel(layer, total_ref, left, right, *refs, block):
    share_refs, total, place_ref = refs[:-2], refs[-2], refs[-1]
    total[...] = total_ref[...]
    add_term(total, place_ref, part(left, block, BLOCK), right)
    half = layer[0] // TRIO
    for turn, share in enumerate(share_refs):
        spot = lax.rem(layer[0] + turn, TRIO)
        for n, side in enumerate((half, 1 - half)):
            rows = pl.ds(pl.multiple_of((side * TRIO + spot) * SHARE, SHARE), SHARE)
            share[n * SHARE : (n + 1) * SHARE, :] = total[rows, :].astype(share.dtype)


def gather_kernel(own, one, two, near, far):
    added = own[...].astype(jnp.float32) + one[...].astype(jnp.float32) + two[...].astype(jnp.float32)
    near[...] = added[:SHARE]
    far[...] = added[SHARE:].astype(far.dtype)


def final_kernel(*refs):
    out_ref = refs[-1]
    for n in range(HELD):
        added = refs[2 * n][...] + refs[2 * n + 1][...].astype(jnp.float32)
        out_ref[:, n * TS : (n + 1) * TS] = added.astype(out_ref.dtype)


AHEAD = 10**10
SMEM = pl.BlockSpec(memory_space=pltpu.SMEM)
VMEM = pl.BlockSpec(memory_space=pltpu.VMEM)
PARAMS = pltpu.CompilerParams(vmem_limit_bytes=32 * 1024 * 1024)


def call(kernel, out_shape, in_specs, operands, scratch=(), cost=0):
    return pl.pallas_call(
        kernel,
        out_shape=out_shape,
        in_specs=in_specs,
        out_specs=jax.tree.map(lambda _: VMEM, out_shape),
        scratch_shapes=scratch,
        compiler_params=PARAMS,
        cost_estimate=pl.CostEstimate(flops=cost, bytes_accessed=0, transcendentals=0),
    )(*operands)


def array(rows, columns, dtype=jnp.bfloat16):
    return jax.ShapeDtypeStruct((rows, columns), dtype)


def body(left_tiles, left_place, right_tiles, right_place):
    layer = lax.axis_index("layer").astype(jnp.int32).reshape(1)
    places = pltpu.SMEM((SA,), jnp.int32)
    sums = [array(RT * TS, TS, jnp.float32)] * HELD
    rights = call(pack_right_kernel, array(HELD * PIECE, TS), [SMEM, VMEM], (right_place[0, 0], right_tiles[0, 0]))
    right_one = shifted(rights, "row", -1)
    lefts, left_zero = call(
        pack_left_kernel,
        [array(HELD * BLOCK, TS), array(BLOCK, TS)],
        [SMEM, VMEM],
        (left_place[0, 0], left_tiles[0, 0]),
    )
    right_two = shifted(rights, "row", -2)
    left_next = shifted(lefts, "col", -1)
    left_last = shifted(left_zero, "col", -2)
    right_one, own = lax.optimization_barrier((right_one, rights))
    totals = call(local_kernel, sums, [VMEM] * 2, (lefts, own), [places], cost=AHEAD)
    totals = call(early_kernel, sums, [VMEM] * (4 + HELD), (lefts, left_next, right_one, right_two, *totals), [places])
    right_three = [shifted(right_one[j * PIECE : (j + 1) * PIECE], "row", -2) for j in range(HELD)]
    held = [(left_next, 1), (left_last, 0)]
    trio = [[(p, p // TRIO * TRIO + (p + turn) % TRIO) for p in range(2 * TRIO)] for turn in range(TRIO)]
    across = [(p, (p + TRIO) % (2 * TRIO)) for p in range(2 * TRIO)]
    shares = []
    for j in range(HELD):
        if j:
            right_three[j], shares[j - 1] = lax.optimization_barrier((right_three[j], shares[j - 1]))
        left, block = held[j]
        shares.append(
            call(
                functools.partial(late_kernel, block=block),
                [array(2 * SHARE, TS)] * TRIO,
                [SMEM] + [VMEM] * 3,
                (layer, totals[j], left, right_three[j]),
                [pltpu.VMEM((RT * TS, TS), jnp.float32), places],
            )
        )
    ends = []
    for j, (own_share, *others) in enumerate(shares):
        arrived = [lax.ppermute(share, "layer", trio[turn]) for turn, share in enumerate(others, 1)]
        if j:
            arrived, ends = lax.optimization_barrier((arrived, ends))
        near, far = call(
            gather_kernel,
            [array(SHARE, TS, jnp.float32), array(SHARE, TS)],
            [VMEM] * TRIO,
            (own_share, *arrived),
            cost=(1 - j) * 10**12,
        )
        ends.append(near)
        shares[j] = far
    for j, far in enumerate(shares):
        ends.insert(2 * j + 1, lax.ppermute(far, "layer", across))
    return call(final_kernel, array(SHARE, HELD * TS), [VMEM] * len(ends), ends)


def solution(mesh):
    return jax.shard_map(
        body,
        mesh=mesh,
        in_specs=(
            P("layer", "row", "col", None, None, None),
            P("layer", "row", "col", None),
            P("layer", "row", "col", None, None, None),
            P("layer", "row", "col", None),
        ),
        out_specs=P(("row", "layer"), "col"),
        check_vma=False,
    )
```

```python
import functools

import jax
import jax.numpy as jnp
from jax import lax
from jax.experimental import pallas as pl
from jax.experimental.pallas import tpu as pltpu
from jax.sharding import PartitionSpec as P

TS = 256
KT = 8
RT = 3
SA = 6
SB = 2
TRIO = 3
SHARE = 128
HELD = 2
NOTE = 16
PIECE = SB * TS + NOTE
BLOCK = SA * TS + NOTE


def shifted(block, axis, distance):
    size = lax.axis_size(axis)
    return lax.ppermute(block, axis, [((i - distance) % size, i) for i in range(size)])


def add_term(total, place_ref, left_ref, right_ref):
    first, second = noted(right_ref, SB)
    for q, place in enumerate(noted(left_ref, SA)):
        place_ref[q] = place

    def slot(q, carry):
        place = place_ref[q]
        inner = lax.rem(place, KT)
        used = place >= 0
        hits_first = used & (first == inner)
        hits_second = used & (second == inner)

        @pl.when(hits_first | hits_second)
        def _():
            left_rows = pl.ds(pl.multiple_of(q * TS, TS), TS)
            right_rows = pl.ds(pl.multiple_of(jnp.where(hits_first, 0, TS), TS), TS)
            rows = pl.ds(pl.multiple_of((place // KT) * TS, TS), TS)
            total[rows, :] += jnp.dot(
                left_ref[left_rows, :], right_ref[right_rows, :], preferred_element_type=jnp.float32
            )

        return carry

    lax.fori_loop(0, SA, slot, 0)


def noted(packed_ref, slots):
    note = packed_ref[slots * TS : slots * TS + NOTE, :128].astype(jnp.float32).astype(jnp.int32)
    return [note[0, p] for p in range(slots)]


def write_note(packed_ref, place_ref, column, slots):
    shape = (NOTE, packed_ref.shape[1])
    lane = lax.broadcasted_iota(jnp.int32, shape, 1)
    note = jnp.full(shape, -1, jnp.int32)
    for p in range(slots):
        note = jnp.where(lane == p, place_ref[column, p], note)
    packed_ref[slots * TS :, :] = note.astype(jnp.float32).astype(jnp.bfloat16)


def pack_right_kernel(place_ref, right_ref, *pieces):
    for column, piece in enumerate(pieces):
        for p in range(SB):
            piece[p * TS : (p + 1) * TS, :] = right_ref[column, p]
        write_note(piece, place_ref, column, SB)


def pack_left_kernel(place_ref, left_ref, right_zero, right_one, lefts, left_zero, rights):
    for column in range(HELD):
        targets = [part(lefts, column, BLOCK)] + [left_zero] * (column == 0)
        for target in targets:
            for q in range(SA):
                target[q * TS : (q + 1) * TS, :] = left_ref[column, q]
            write_note(target, place_ref, column, SA)
    rights[:PIECE, :] = right_zero[...]
    rights[PIECE:, :] = right_one[...]


def part(ref, column, rows):
    return ref.at[column * rows : (column + 1) * rows]


def mark_kernel(right_one, mark):
    mark[...] = jnp.zeros_like(mark)


def local_kernel(lefts, rights, *refs):
    totals, place_ref = refs[:-1], refs[-1]
    for column, total in enumerate(totals):
        total[...] = jnp.zeros_like(total)
        add_term(total, place_ref, part(lefts, column, BLOCK), part(rights, column, PIECE))


def middle_kernel(mark, start, left_one, right_one, left_two, right_two, total, place_ref, *, column):
    total[...] = start[...]
    add_term(total, place_ref, part(left_one, 1 - column, BLOCK), right_one)
    add_term(total, place_ref, part(left_two, column, BLOCK), part(right_two, column, PIECE))


def late_kernel(layer, total_ref, left, right, *refs, block):
    share_refs, total, place_ref = refs[:-2], refs[-2], refs[-1]
    total[...] = total_ref[...]
    add_term(total, place_ref, part(left, block, BLOCK), right)
    half = layer[0] // TRIO
    for turn, share in enumerate(share_refs):
        spot = lax.rem(layer[0] + turn, TRIO)
        for n, side in enumerate((half, 1 - half)):
            rows = pl.ds(pl.multiple_of((side * TRIO + spot) * SHARE, SHARE), SHARE)
            share[n * SHARE : (n + 1) * SHARE, :] = total[rows, :].astype(share.dtype)


def gather_kernel(own, one, two, near, far):
    added = own[...].astype(jnp.float32) + one[...].astype(jnp.float32) + two[...].astype(jnp.float32)
    near[...] = added[:SHARE]
    far[...] = added[SHARE:].astype(far.dtype)


def final_kernel(*refs):
    out_ref = refs[-1]
    for n in range(HELD):
        added = refs[2 * n][...] + refs[2 * n + 1][...].astype(jnp.float32)
        out_ref[:, n * TS : (n + 1) * TS] = added.astype(out_ref.dtype)


AHEAD = 4 * 10**10
SMEM = pl.BlockSpec(memory_space=pltpu.SMEM)
VMEM = pl.BlockSpec(memory_space=pltpu.VMEM)
ANY = pl.BlockSpec(memory_space=pl.ANY)
PARAMS = pltpu.CompilerParams(vmem_limit_bytes=32 * 1024 * 1024)


def call(kernel, out_shape, in_specs, operands, scratch=(), cost=0):
    return pl.pallas_call(
        kernel,
        out_shape=out_shape,
        in_specs=in_specs,
        out_specs=jax.tree.map(lambda _: VMEM, out_shape),
        scratch_shapes=scratch,
        compiler_params=PARAMS,
        cost_estimate=pl.CostEstimate(flops=cost, bytes_accessed=0, transcendentals=0),
    )(*operands)


def array(rows, columns, dtype=jnp.bfloat16):
    return jax.ShapeDtypeStruct((rows, columns), dtype)


def body(left_tiles, left_place, right_tiles, right_place):
    layer = lax.axis_index("layer").astype(jnp.int32).reshape(1)
    places = pltpu.SMEM((SA,), jnp.int32)
    total = array(RT * TS, TS, jnp.float32)
    pieces = call(pack_right_kernel, [array(PIECE, TS)] * HELD, [SMEM, VMEM], (right_place[0, 0], right_tiles[0, 0]))
    right_one = [shifted(piece, "row", -1) for piece in pieces]
    lefts, left_zero, rights = call(
        pack_left_kernel,
        [array(HELD * BLOCK, TS), array(BLOCK, TS), array(HELD * PIECE, TS)],
        [SMEM] + [VMEM] * 3,
        (left_place[0, 0], left_tiles[0, 0], *pieces),
    )
    right_two = shifted(rights, "row", -2)
    left_next = shifted(lefts, "col", -1)
    left_last = shifted(left_zero, "col", -2)
    totals = list(call(local_kernel, [total] * HELD, [VMEM] * 2, (lefts, rights), [places]))
    right_one[0], totals = lax.optimization_barrier((right_one[0], totals))
    mark = call(mark_kernel, array(8, 128, jnp.float32), [ANY], (right_one[1],), cost=AHEAD)
    right_two, left_next, left_last, mark = lax.optimization_barrier((right_two, left_next, left_last, mark))
    right_three = [shifted(piece, "row", -2) for piece in right_one]
    ones, held = (lefts, left_next), ((left_next, 1), (left_last, 0))
    trio = [[(p, p // TRIO * TRIO + (p + turn) % TRIO) for p in range(2 * TRIO)] for turn in range(TRIO)]
    across = [(p, (p + TRIO) % (2 * TRIO)) for p in range(2 * TRIO)]
    shares = []
    for j in range(HELD):
        if j:
            totals[j], shares[j - 1] = lax.optimization_barrier((totals[j], shares[j - 1]))
        left, block = held[j]
        start = call(
            functools.partial(middle_kernel, column=j),
            total,
            [ANY] + [VMEM] * 5,
            (mark, totals[j], ones[j], right_one[j], left_next, right_two),
            [places],
        )
        if j:
            right_three[j], start = lax.optimization_barrier((right_three[j], start))
        shares.append(
            call(
                functools.partial(late_kernel, block=block),
                [array(2 * SHARE, TS)] * TRIO,
                [SMEM] + [VMEM] * 3,
                (layer, start, left, right_three[j]),
                [pltpu.VMEM((RT * TS, TS), jnp.float32), places],
            )
        )
    ends = []
    for j, (own_share, *others) in enumerate(shares):
        arrived = [lax.ppermute(share, "layer", trio[turn]) for turn, share in enumerate(others, 1)]
        if j:
            arrived, ends = lax.optimization_barrier((arrived, ends))
        near, far = call(
            gather_kernel,
            [array(SHARE, TS, jnp.float32), array(SHARE, TS)],
            [VMEM] * TRIO,
            (own_share, *arrived),
            cost=(1 - j) * 10**12,
        )
        ends.append(near)
        shares[j] = far
    for j, far in enumerate(shares):
        ends.insert(2 * j + 1, lax.ppermute(far, "layer", across))
    return call(final_kernel, array(SHARE, HELD * TS), [VMEM] * len(ends), ends)


def solution(mesh):
    return jax.shard_map(
        body,
        mesh=mesh,
        in_specs=(
            P("layer", "row", "col", None, None, None),
            P("layer", "row", "col", None),
            P("layer", "row", "col", None, None, None),
            P("layer", "row", "col", None),
        ),
        out_specs=P(("row", "layer"), "col"),
        check_vma=False,
    )
```

```python
import functools

import jax
import jax.numpy as jnp
from jax import lax
from jax.experimental import pallas as pl
from jax.experimental.pallas import tpu as pltpu
from jax.sharding import PartitionSpec as P

TS = 256
KT = 8
RT = 3
SA = 6
SB = 2
TRIO = 3
SHARE = 128
HELD = 2
NOTE = 16
PIECE = SB * TS + NOTE
BLOCK = SA * TS + NOTE


def shifted(block, axis, distance):
    size = lax.axis_size(axis)
    return lax.ppermute(block, axis, [((i - distance) % size, i) for i in range(size)])


def add_term(total, place_ref, left_ref, right_ref):
    first, second = noted(right_ref, SB)
    for q, place in enumerate(noted(left_ref, SA)):
        place_ref[q] = place

    def slot(q, carry):
        place = place_ref[q]
        inner = lax.rem(place, KT)
        used = place >= 0
        hits_first = used & (first == inner)
        hits_second = used & (second == inner)

        @pl.when(hits_first | hits_second)
        def _():
            left_rows = pl.ds(pl.multiple_of(q * TS, TS), TS)
            right_rows = pl.ds(pl.multiple_of(jnp.where(hits_first, 0, TS), TS), TS)
            rows = pl.ds(pl.multiple_of((place // KT) * TS, TS), TS)
            total[rows, :] += jnp.dot(
                left_ref[left_rows, :], right_ref[right_rows, :], preferred_element_type=jnp.float32
            )

        return carry

    lax.fori_loop(0, SA, slot, 0)


def noted(packed_ref, slots):
    note = packed_ref[slots * TS : slots * TS + NOTE, :128].astype(jnp.float32).astype(jnp.int32)
    return [note[0, p] for p in range(slots)]


def write_note(packed_ref, place_ref, column, slots):
    shape = (NOTE, packed_ref.shape[1])
    lane = lax.broadcasted_iota(jnp.int32, shape, 1)
    note = jnp.full(shape, -1, jnp.int32)
    for p in range(slots):
        note = jnp.where(lane == p, place_ref[column, p], note)
    packed_ref[slots * TS :, :] = note.astype(jnp.float32).astype(jnp.bfloat16)


def pack(copies, place_ref, notes, sem):
    copies = [pltpu.make_async_copy(source, target, sem.at[n]) for n, (source, target) in enumerate(copies)]
    for copy in copies:
        copy.start()
    for packed, column, slots in notes:
        write_note(packed, place_ref, column, slots)
    for copy in copies:
        copy.wait()


def pack_right_kernel(place_ref, right_ref, *refs):
    pieces, sem = refs[:-1], refs[-1]
    copies = [
        (right_ref.at[column, p], piece.at[p * TS : (p + 1) * TS]) for column, piece in enumerate(pieces) for p in range(SB)
    ]
    pack(copies, place_ref, [(piece, column, SB) for column, piece in enumerate(pieces)], sem)


def pack_left_kernel(right_place, left_place, right_ref, left_ref, lefts, left_zero, rights, sem):
    copies = []
    for column in range(HELD):
        for target in [part(lefts, column, BLOCK)] + [left_zero] * (column == 0):
            copies += [(left_ref.at[column, q], target.at[q * TS : (q + 1) * TS]) for q in range(SA)]
        target = part(rights, column, PIECE)
        copies += [(right_ref.at[column, p], target.at[p * TS : (p + 1) * TS]) for p in range(SB)]
    notes = [(part(lefts, column, BLOCK), column, SA) for column in range(HELD)] + [(left_zero, 0, SA)]
    pack(copies, left_place, notes, sem)
    for column in range(HELD):
        write_note(part(rights, column, PIECE), right_place, column, SB)


def part(ref, column, rows):
    return ref.at[column * rows : (column + 1) * rows]


def mark_kernel(right_one, mark):
    mark[...] = jnp.zeros_like(mark)


def local_kernel(lefts, rights, *refs):
    totals, place_ref = refs[:-1], refs[-1]
    for column, total in enumerate(totals):
        total[...] = jnp.zeros_like(total)
        add_term(total, place_ref, part(lefts, column, BLOCK), part(rights, column, PIECE))


def middle_kernel(mark, start, left_one, right_one, left_two, right_two, total, place_ref, *, column):
    total[...] = start[...]
    add_term(total, place_ref, part(left_one, 1 - column, BLOCK), right_one)
    add_term(total, place_ref, part(left_two, column, BLOCK), part(right_two, column, PIECE))


def late_kernel(layer, total_ref, left, right, *refs, block):
    share_refs, total, place_ref = refs[:-2], refs[-2], refs[-1]
    total[...] = total_ref[...]
    add_term(total, place_ref, part(left, block, BLOCK), right)
    half = layer[0] // TRIO
    for turn, share in enumerate(share_refs):
        spot = lax.rem(layer[0] + turn, TRIO)
        for n, side in enumerate((half, 1 - half)):
            rows = pl.ds(pl.multiple_of((side * TRIO + spot) * SHARE, SHARE), SHARE)
            share[n * SHARE : (n + 1) * SHARE, :] = total[rows, :].astype(share.dtype)


def add_trio(own, one, two):
    return own[...].astype(jnp.float32) + one[...].astype(jnp.float32) + two[...].astype(jnp.float32)


def gather_kernel(own, one, two, added):
    added[...] = add_trio(own, one, two)


def join_kernel(first, own, one, two, near, far):
    for column, added in enumerate((first[...], add_trio(own, one, two))):
        near[:, column * TS : (column + 1) * TS] = added[:SHARE]
        far[:, column * TS : (column + 1) * TS] = added[SHARE:].astype(far.dtype)


def final_kernel(near, far, out_ref):
    out_ref[...] = (near[...] + far[...].astype(jnp.float32)).astype(out_ref.dtype)


AHEAD = 4 * 10**10
SMEM = pl.BlockSpec(memory_space=pltpu.SMEM)
VMEM = pl.BlockSpec(memory_space=pltpu.VMEM)
ANY = pl.BlockSpec(memory_space=pl.ANY)
HBM = pl.BlockSpec(memory_space=pltpu.HBM)
PARAMS = pltpu.CompilerParams(vmem_limit_bytes=8 * 1024 * 1024)


def call(kernel, out_shape, in_specs, operands, scratch=(), cost=0):
    return pl.pallas_call(
        kernel,
        out_shape=out_shape,
        in_specs=in_specs,
        out_specs=jax.tree.map(lambda _: VMEM, out_shape),
        scratch_shapes=scratch,
        compiler_params=PARAMS,
        cost_estimate=pl.CostEstimate(flops=cost, bytes_accessed=0, transcendentals=0),
    )(*operands)


def array(rows, columns, dtype=jnp.bfloat16):
    return jax.ShapeDtypeStruct((rows, columns), dtype)


def body(left_tiles, left_place, right_tiles, right_place):
    layer = lax.axis_index("layer").astype(jnp.int32).reshape(1)
    places = pltpu.SMEM((SA,), jnp.int32)
    total = array(RT * TS, TS, jnp.float32)
    right_at, right = right_place[0, 0], right_tiles[0, 0]
    pieces = call(
        pack_right_kernel,
        [array(PIECE, TS)] * HELD,
        [SMEM, HBM],
        (right_at, right),
        [pltpu.SemaphoreType.DMA((HELD * SB,))],
    )
    right_one = [shifted(piece, "row", -1) for piece in pieces]
    left_at, left, right_at, right, pieces = lax.optimization_barrier((left_place[0, 0], left_tiles[0, 0], right_at, right, pieces))
    lefts, left_zero, rights = call(
        pack_left_kernel,
        [array(HELD * BLOCK, TS), array(BLOCK, TS), array(HELD * PIECE, TS)],
        [SMEM] * 2 + [HBM] * 2,
        (right_at, left_at, right, left),
        [pltpu.SemaphoreType.DMA((HELD * (SA + SB) + SA,))],
    )
    right_two = shifted(rights, "row", -2)
    left_next = shifted(lefts, "col", -1)
    left_last = shifted(left_zero, "col", -2)
    totals = list(call(local_kernel, [total] * HELD, [VMEM] * 2, (lefts, rights), [places]))
    right_one[0], totals = lax.optimization_barrier((right_one[0], totals))
    mark = call(mark_kernel, array(8, 128, jnp.float32), [ANY], (right_one[1],), cost=AHEAD)
    right_two, left_next, mark = lax.optimization_barrier((right_two, left_next, mark))
    right_three = [shifted(piece, "row", -2) for piece in right_one]
    ones, held = (lefts, left_next), ((left_next, 1), (left_last, 0))
    trio = [[(p, p // TRIO * TRIO + (p + turn) % TRIO) for p in range(2 * TRIO)] for turn in range(TRIO)]
    across = [(p, (p + TRIO) % (2 * TRIO)) for p in range(2 * TRIO)]
    shares = []
    for j in range(HELD):
        if j:
            totals[j], shares[j - 1] = lax.optimization_barrier((totals[j], shares[j - 1]))
        left, block = held[j]
        start = call(
            functools.partial(middle_kernel, column=j),
            total,
            [ANY] + [VMEM] * 5,
            (mark, totals[j], ones[j], right_one[j], left_next, right_two),
            [places],
        )
        if j:
            right_three[j], start = lax.optimization_barrier((right_three[j], start))
        shares.append(
            call(
                functools.partial(late_kernel, block=block),
                [array(2 * SHARE, TS)] * TRIO,
                [SMEM] + [VMEM] * 3,
                (layer, start, left, right_three[j]),
                [pltpu.VMEM((RT * TS, TS), jnp.float32), places],
            )
        )
    arrived = [
        [own] + [lax.ppermute(share, "layer", trio[turn]) for turn, share in enumerate(others, 1)] for own, *others in shares
    ]
    first = call(gather_kernel, array(2 * SHARE, TS, jnp.float32), [VMEM] * TRIO, arrived[0], cost=10**12)
    first, *second = lax.optimization_barrier((first, *arrived[1]))
    near, far = call(
        join_kernel,
        [array(SHARE, HELD * TS, jnp.float32), array(SHARE, HELD * TS)],
        [VMEM] * (1 + TRIO),
        (first, *second),
    )
    return call(final_kernel, array(SHARE, HELD * TS), [VMEM] * 2, (near, lax.ppermute(far, "layer", across)))


def solution(mesh):
    return jax.shard_map(
        body,
        mesh=mesh,
        in_specs=(
            P("layer", "row", "col", None, None, None),
            P("layer", "row", "col", None),
            P("layer", "row", "col", None, None, None),
            P("layer", "row", "col", None),
        ),
        out_specs=P(("row", "layer"), "col"),
        check_vma=False,
    )
```

```python
import functools

import jax
import jax.numpy as jnp
from jax import lax
from jax.experimental import pallas as pl
from jax.experimental.pallas import tpu as pltpu
from jax.sharding import PartitionSpec as P

TS = 256
KT = 8
RT = 3
SA = 6
SB = 2
STEPS = 4
TRIO = 3
SHARE = 128
HELD = 2
NOTE = 16
PIECE = SB * TS + NOTE
BLOCK = SA * TS + NOTE


def shifted(block, axis, distance):
    size = lax.axis_size(axis)
    return lax.ppermute(block, axis, [((i - distance) % size, i) for i in range(size)])


def add_term(total, place_ref, left_ref, right_ref):
    first, second = noted(right_ref, SB)
    for q, place in enumerate(noted(left_ref, SA)):
        place_ref[q] = place

    def slot(q, carry):
        place = place_ref[q]
        inner = lax.rem(place, KT)
        used = place >= 0
        hits_first = used & (first == inner)
        hits_second = used & (second == inner)

        @pl.when(hits_first | hits_second)
        def _():
            left_rows = pl.ds(pl.multiple_of(q * TS, TS), TS)
            right_rows = pl.ds(pl.multiple_of(jnp.where(hits_first, 0, TS), TS), TS)
            rows = pl.ds(pl.multiple_of((place // KT) * TS, TS), TS)
            total[rows, :] += jnp.dot(
                left_ref[left_rows, :], right_ref[right_rows, :], preferred_element_type=jnp.float32
            )

        return carry

    lax.fori_loop(0, SA, slot, 0)


def noted(packed_ref, slots):
    note = packed_ref[slots * TS : slots * TS + NOTE, :128].astype(jnp.float32).astype(jnp.int32)
    return [note[0, p] for p in range(slots)]


def write_note(packed_ref, place_ref, column, slots):
    shape = (NOTE, packed_ref.shape[1])
    lane = lax.broadcasted_iota(jnp.int32, shape, 1)
    note = jnp.full(shape, -1, jnp.int32)
    for p in range(slots):
        note = jnp.where(lane == p, place_ref[column, p], note)
    packed_ref[slots * TS :, :] = note.astype(jnp.float32).astype(jnp.bfloat16)


def pack_right_kernel(place_ref, right_ref, *pieces):
    for column, piece in enumerate(pieces):
        for p in range(SB):
            piece[p * TS : (p + 1) * TS, :] = right_ref[column, p]
        write_note(piece, place_ref, column, SB)


def pack_left_kernel(place_ref, left_ref, right_zero, right_one, lefts, left_zero, rights):
    for column in range(HELD):
        targets = [part(lefts, column, BLOCK)] + [left_zero] * (column == 0)
        for target in targets:
            for q in range(SA):
                target[q * TS : (q + 1) * TS, :] = left_ref[column, q]
            write_note(target, place_ref, column, SA)
    rights[:PIECE, :] = right_zero[...]
    rights[PIECE:, :] = right_one[...]


def part(ref, column, rows):
    return ref.at[column * rows : (column + 1) * rows]


def mark_kernel(right_one, mark):
    mark[...] = jnp.zeros_like(mark)


def block_kernel(layer, mark, lefts, left_next, *refs, column):
    count = STEPS + column
    arriving, shares = list(refs[:count]), refs[count : count + TRIO]
    arriving[2] = part(arriving[2], column, PIECE)
    total, place_ref, pieces, last, sem = refs[count + TRIO :]
    targets = [pieces.at[step] for step in range(STEPS)] + [last] * column
    copies = [pltpu.make_async_copy(source, target, sem.at[n]) for n, (source, target) in enumerate(zip(arriving, targets))]
    for copy in copies:
        copy.start()
    blocks = [part(lefts, 0, BLOCK), part(lefts, 1, BLOCK), part(left_next, 0, BLOCK), part(left_next, 1, BLOCK), last]
    total[...] = jnp.zeros_like(total)
    for step in range(STEPS):
        copies[step].wait()
        if column and step == STEPS - 1:
            copies[STEPS].wait()
        add_term(total, place_ref, blocks[column + step], pieces.at[step])
    half = layer[0] // TRIO
    for turn, share in enumerate(shares):
        spot = lax.rem(layer[0] + turn, TRIO)
        for n, side in enumerate((half, 1 - half)):
            rows = pl.ds(pl.multiple_of((side * TRIO + spot) * SHARE, SHARE), SHARE)
            share[n * SHARE : (n + 1) * SHARE, :] = total[rows, :].astype(share.dtype)


def gather_kernel(own, one, two, near, far):
    added = own[...].astype(jnp.float32) + one[...].astype(jnp.float32) + two[...].astype(jnp.float32)
    near[...] = added[:SHARE]
    far[...] = added[SHARE:].astype(far.dtype)


def total_kernel(near, far, out_ref):
    out_ref[...] = (near[...] + far[...].astype(jnp.float32)).astype(out_ref.dtype)


def final_kernel(first, near, far, out_ref):
    out_ref[:, :TS] = first[...]
    total_kernel(near, far, out_ref.at[:, TS:])


AHEAD = 4 * 10**10
GATHER = 10**12
FIRST = 10**12
AFTER = 0
SMEM = pl.BlockSpec(memory_space=pltpu.SMEM)
VMEM = pl.BlockSpec(memory_space=pltpu.VMEM)
ANY = pl.BlockSpec(memory_space=pl.ANY)
PARAMS = pltpu.CompilerParams(vmem_limit_bytes=12 * 1024 * 1024)


def call(kernel, out_shape, in_specs, operands, scratch=(), cost=0):
    return pl.pallas_call(
        kernel,
        out_shape=out_shape,
        in_specs=in_specs,
        out_specs=jax.tree.map(lambda _: VMEM, out_shape),
        scratch_shapes=scratch,
        compiler_params=PARAMS,
        cost_estimate=pl.CostEstimate(flops=cost, bytes_accessed=0, transcendentals=0),
    )(*operands)


def array(rows, columns, dtype=jnp.bfloat16):
    return jax.ShapeDtypeStruct((rows, columns), dtype)


def body(left_tiles, left_place, right_tiles, right_place):
    layer = lax.axis_index("layer").astype(jnp.int32).reshape(1)
    pieces = call(pack_right_kernel, [array(PIECE, TS)] * HELD, [SMEM, VMEM], (right_place[0, 0], right_tiles[0, 0]))
    right_one = [shifted(piece, "row", -1) for piece in pieces]
    lefts, left_zero, rights = call(
        pack_left_kernel,
        [array(HELD * BLOCK, TS), array(BLOCK, TS), array(HELD * PIECE, TS)],
        [SMEM] + [VMEM] * 3,
        (left_place[0, 0], left_tiles[0, 0], *pieces),
    )
    right_two = shifted(rights, "row", -2)
    left_next = shifted(lefts, "col", -1)
    left_last = shifted(left_zero, "col", -2)
    mark = call(mark_kernel, array(8, 128, jnp.float32), [ANY], (right_one[1],), cost=AHEAD)
    right_two, left_next, mark = lax.optimization_barrier((right_two, left_next, mark))
    right_three = [shifted(piece, "row", -2) for piece in right_one]
    trio = [[(p, p // TRIO * TRIO + (p + turn) % TRIO) for p in range(2 * TRIO)] for turn in range(TRIO)]
    across = [(p, (p + TRIO) % (2 * TRIO)) for p in range(2 * TRIO)]
    shares = []
    for j in range(HELD):
        arriving = [pieces[j], right_one[j], right_two, right_three[j]] + [left_last] * j
        if j:
            arriving[0], shares[j - 1] = lax.optimization_barrier((arriving[0], shares[j - 1]))
        shares.append(
            call(
                functools.partial(block_kernel, column=j),
                [array(2 * SHARE, TS)] * TRIO,
                [SMEM, ANY] + [VMEM] * 2 + [ANY] * len(arriving),
                (layer, mark, lefts, left_next, *arriving),
                [
                    pltpu.VMEM((RT * TS, TS), jnp.float32),
                    pltpu.SMEM((SA,), jnp.int32),
                    pltpu.VMEM((STEPS, PIECE, TS), jnp.bfloat16),
                    pltpu.VMEM((BLOCK, TS), jnp.bfloat16),
                    pltpu.SemaphoreType.DMA((STEPS + 1,)),
                ],
            )
        )
    ends = []
    for j, (own, *others) in enumerate(shares):
        arrived = [lax.ppermute(share, "layer", trio[turn]) for turn, share in enumerate(others, 1)]
        if j:
            arrived, ends = lax.optimization_barrier((arrived, ends))
        near, far = call(
            gather_kernel,
            [array(SHARE, TS, jnp.float32), array(SHARE, TS)],
            [VMEM] * TRIO,
            (own, *arrived),
            cost=(GATHER, AFTER)[j],
        )
        ends.append(near)
        shares[j] = lax.ppermute(far, "layer", across)
    first = call(total_kernel, array(SHARE, TS), [VMEM] * 2, (ends[0], shares[0]), cost=FIRST)
    return call(final_kernel, array(SHARE, HELD * TS), [VMEM] * 3, (first, ends[1], shares[1]))


def solution(mesh):
    return jax.shard_map(
        body,
        mesh=mesh,
        in_specs=(
            P("layer", "row", "col", None, None, None),
            P("layer", "row", "col", None),
            P("layer", "row", "col", None, None, None),
            P("layer", "row", "col", None),
        ),
        out_specs=P(("row", "layer"), "col"),
        check_vma=False,
    )
```

```python
import jax
import jax.numpy as jnp
from jax import lax
from jax.experimental import pallas as pl
from jax.experimental.pallas import tpu as pltpu
from jax.sharding import PartitionSpec as P

TS = 256
KT = 8
RT = 3
SA = 6
SB = 2
STEPS = 4
TRIO = 3
SHARE = 128
HELD = 2
NOTE = 16
PIECE = SB * TS + NOTE
BLOCK = SA * TS + NOTE


def shifted(block, axis, distance):
    size = lax.axis_size(axis)
    return lax.ppermute(block, axis, [((i - distance) % size, i) for i in range(size)])


def add_term(total, place_ref, left_ref, right_ref):
    first, second = noted(right_ref, SB)
    for q, place in enumerate(noted(left_ref, SA)):
        place_ref[q] = place

    def slot(q, carry):
        place = place_ref[q]
        inner = lax.rem(place, KT)
        used = place >= 0
        hits_first = used & (first == inner)
        hits_second = used & (second == inner)

        @pl.when(hits_first | hits_second)
        def _():
            left_rows = pl.ds(pl.multiple_of(q * TS, TS), TS)
            right_rows = pl.ds(pl.multiple_of(jnp.where(hits_first, 0, TS), TS), TS)
            rows = pl.ds(pl.multiple_of((place // KT) * TS, TS), TS)
            total[rows, :] += jnp.dot(
                left_ref[left_rows, :], right_ref[right_rows, :], preferred_element_type=jnp.float32
            )

        return carry

    lax.fori_loop(0, SA, slot, 0)


def noted(packed_ref, slots):
    note = packed_ref[slots * TS : slots * TS + NOTE, :128].astype(jnp.float32).astype(jnp.int32)
    return [note[0, p] for p in range(slots)]


def write_note(packed_ref, place_ref, column, slots):
    shape = (NOTE, packed_ref.shape[1])
    lane = lax.broadcasted_iota(jnp.int32, shape, 1)
    note = jnp.full(shape, -1, jnp.int32)
    for p in range(slots):
        note = jnp.where(lane == p, place_ref[column, p], note)
    packed_ref[slots * TS :, :] = note.astype(jnp.float32).astype(jnp.bfloat16)


def packed(tiles, places):
    count = places.shape[0]
    note = jnp.pad(places.astype(jnp.bfloat16)[None], ((0, NOTE - 1), (0, TS - count)))
    return jnp.concatenate([tiles.reshape(count * TS, TS), note])


def pack_left_kernel(place_ref, left_ref, right_zero, right_one, lefts, left_zero, rights):
    for column in range(HELD):
        targets = [part(lefts, column, BLOCK)] + [left_zero] * (column == 0)
        for target in targets:
            for q in range(SA):
                target[q * TS : (q + 1) * TS, :] = left_ref[column, q]
            write_note(target, place_ref, column, SA)
    rights[:PIECE, :] = right_zero[...]
    rights[PIECE:, :] = right_one[...]


def part(ref, column, rows):
    return ref.at[column * rows : (column + 1) * rows]


def mark_kernel(right_one, mark):
    mark[...] = jnp.zeros_like(mark)


def add_steps(total, place_ref, lefts, left_next, arriving, pieces, last, sem, column):
    arriving = [*arriving[:2], part(arriving[2], column, PIECE), *arriving[3:]]
    targets = [pieces.at[step] for step in range(STEPS)] + [last] * column
    copies = [pltpu.make_async_copy(source, target, sem.at[n]) for n, (source, target) in enumerate(zip(arriving, targets))]
    for copy in copies:
        copy.start()
    blocks = [part(lefts, 0, BLOCK), part(lefts, 1, BLOCK), part(left_next, 0, BLOCK), part(left_next, 1, BLOCK), last]
    total[...] = jnp.zeros_like(total)
    for step in range(STEPS):
        copies[step].wait()
        if column and step == STEPS - 1:
            copies[STEPS].wait()
        add_term(total, place_ref, blocks[column + step], pieces.at[step])


def first_kernel(layer, mark, lefts, left_next, own, one, two, three, keep, send, total, *scratch):
    add_steps(total, scratch[0], lefts, left_next, [own, one, two, three], *scratch[1:], 0)
    pair, side = layer[0] // 2, lax.rem(layer[0], 2)
    for turn in range(TRIO):
        spot = lax.rem(pair + turn, TRIO)
        for share, parity in ((keep, side), (send, 1 - side)):
            rows = pl.ds(pl.multiple_of((2 * spot + parity) * SHARE, SHARE), SHARE)
            share[turn * SHARE : (turn + 1) * SHARE, :] = total[rows, :].astype(share.dtype)


def second_kernel(mark, lefts, left_next, own, one, two, three, left_last, shares, total, *scratch):
    add_steps(total, scratch[0], lefts, left_next, [own, one, two, three, left_last], *scratch[1:], 1)
    shares[...] = total[...].astype(shares.dtype)


def pair_kernel(keep, came, near, *far):
    added = keep[...].astype(jnp.float32) + came[...].astype(jnp.float32)
    near[...] = added[:SHARE]
    for n, share in enumerate(far, 1):
        share[...] = added[n * SHARE : (n + 1) * SHARE].astype(share.dtype)


def final_kernel(near, one, two, shares, out_ref):
    out_ref[:, :TS] = (near[...] + one[...].astype(jnp.float32) + two[...].astype(jnp.float32)).astype(out_ref.dtype)
    total = shares[:SHARE].astype(jnp.float32)
    for n in range(1, 2 * TRIO):
        total += shares[n * SHARE : (n + 1) * SHARE].astype(jnp.float32)
    out_ref[:, TS:] = total.astype(out_ref.dtype)


AHEAD = 4 * 10**10
GATHER = 10**12
SMEM = pl.BlockSpec(memory_space=pltpu.SMEM)
VMEM = pl.BlockSpec(memory_space=pltpu.VMEM)
ANY = pl.BlockSpec(memory_space=pl.ANY)
PARAMS = pltpu.CompilerParams(vmem_limit_bytes=12 * 1024 * 1024)


def call(kernel, out_shape, in_specs, operands, scratch=(), cost=0):
    return pl.pallas_call(
        kernel,
        out_shape=out_shape,
        in_specs=in_specs,
        out_specs=jax.tree.map(lambda _: VMEM, out_shape),
        scratch_shapes=scratch,
        compiler_params=PARAMS,
        cost_estimate=pl.CostEstimate(flops=cost, bytes_accessed=0, transcendentals=0),
    )(*operands)


def array(rows, columns, dtype=jnp.bfloat16):
    return jax.ShapeDtypeStruct((rows, columns), dtype)


def body(left_tiles, left_place, right_tiles, right_place):
    layer = lax.axis_index("layer").astype(jnp.int32).reshape(1)
    right, right_at = right_tiles[0, 0], right_place[0, 0]
    pieces = [packed(right[j], right_at[j]) for j in range(HELD)]
    right_one = [shifted(piece, "row", -1) for piece in pieces]
    lefts, left_zero, rights = call(
        pack_left_kernel,
        [array(HELD * BLOCK, TS), array(BLOCK, TS), array(HELD * PIECE, TS)],
        [SMEM] + [VMEM] * 3,
        (left_place[0, 0], left_tiles[0, 0], *pieces),
    )
    right_two = shifted(rights, "row", -2)
    left_next = shifted(lefts, "col", -1)
    left_last = shifted(left_zero, "col", -2)
    mark = call(mark_kernel, array(8, 128, jnp.float32), [ANY], (right_one[1],), cost=AHEAD)
    right_two, left_next, mark = lax.optimization_barrier((right_two, left_next, mark))
    right_three = [shifted(piece, "row", -2) for piece in right_one]
    scratch = [
        pltpu.VMEM((RT * TS, TS), jnp.float32),
        pltpu.SMEM((SA,), jnp.int32),
        pltpu.VMEM((STEPS, PIECE, TS), jnp.bfloat16),
        pltpu.VMEM((BLOCK, TS), jnp.bfloat16),
        pltpu.SemaphoreType.DMA((STEPS + 1,)),
    ]
    keep, send = call(
        first_kernel,
        [array(TRIO * SHARE, TS)] * 2,
        [SMEM, ANY] + [VMEM] * 2 + [ANY] * STEPS,
        (layer, mark, lefts, left_next, pieces[0], right_one[0], right_two, right_three[0]),
        scratch,
    )
    came = lax.ppermute(send, "layer", [(p, p ^ 1) for p in range(2 * TRIO)])
    pieces[1], send = lax.optimization_barrier((pieces[1], send))
    shares = call(
        second_kernel,
        array(RT * TS, TS),
        [ANY] + [VMEM] * 2 + [ANY] * (STEPS + 1),
        (mark, lefts, left_next, pieces[1], right_one[1], right_two, right_three[1], left_last),
        scratch,
    )
    shares = lax.all_to_all(shares.reshape(2 * TRIO, SHARE, TS), "layer", 0, 0, tiled=True).reshape(RT * TS, TS)
    near, *far = call(
        pair_kernel,
        [array(SHARE, TS, jnp.float32)] + [array(SHARE, TS)] * 2,
        [VMEM] * 2,
        (keep, came),
        cost=GATHER,
    )
    ends = [
        lax.ppermute(share, "layer", [(p, 2 * ((p // 2 + turn) % TRIO) + p % 2) for p in range(2 * TRIO)])
        for turn, share in enumerate(far, 1)
    ]
    return call(final_kernel, array(SHARE, HELD * TS), [VMEM] * 4, (near, *ends, shares))


def solution(mesh):
    return jax.shard_map(
        body,
        mesh=mesh,
        in_specs=(
            P("layer", "row", "col", None, None, None),
            P("layer", "row", "col", None),
            P("layer", "row", "col", None, None, None),
            P("layer", "row", "col", None),
        ),
        out_specs=P(("row", "layer"), "col"),
        check_vma=False,
    )
```

```python
import functools

import jax
import jax.numpy as jnp
from jax import lax
from jax.experimental import pallas as pl
from jax.experimental.pallas import tpu as pltpu
from jax.sharding import PartitionSpec as P

TS = 256
KT = 8
RT = 3
SA = 6
SB = 2
STEPS = 4
TRIO = 3
SHARE = 128
HELD = 2
NOTE = 16
PIECE = SB * TS + NOTE
BLOCK = SA * TS + NOTE


def shifted(block, axis, distance):
    size = lax.axis_size(axis)
    return lax.ppermute(block, axis, [((i - distance) % size, i) for i in range(size)])


def add_term(total, hit_ref, left_ref, right_ref):
    first, second = noted(right_ref, SB)
    left_places = noted(left_ref, SA)
    count = jnp.int32(0)
    for q in range(SA):
        place = left_places[q]
        inner = lax.rem(place, KT)
        hits_first = first == inner
        hit = (place >= 0) & (hits_first | (second == inner))

        @pl.when(hit)
        def _():
            hit_ref[0, count] = q * TS
            hit_ref[1, count] = jnp.where(hits_first, 0, TS)
            hit_ref[2, count] = (place // KT) * TS

        count = count + hit.astype(jnp.int32)

    def product(n, carry):
        left_rows, right_rows, rows = (pl.ds(pl.multiple_of(hit_ref[k, n], TS), TS) for k in range(3))
        total[rows, :] += jnp.dot(left_ref[left_rows, :], right_ref[right_rows, :], preferred_element_type=jnp.float32)
        return carry

    lax.fori_loop(0, count, product, 0)


def noted(packed_ref, slots):
    note = packed_ref[slots * TS : slots * TS + NOTE, :128].astype(jnp.float32).astype(jnp.int32)
    return [note[0, p] for p in range(slots)]


def write_note(packed_ref, place_ref, column, slots):
    shape = (NOTE, packed_ref.shape[1])
    lane = lax.broadcasted_iota(jnp.int32, shape, 1)
    note = jnp.full(shape, -1, jnp.int32)
    for p in range(slots):
        note = jnp.where(lane == p, place_ref[column, p], note)
    packed_ref[slots * TS :, :] = note.astype(jnp.float32).astype(jnp.bfloat16)


def packed(tiles, places):
    count = places.shape[0]
    note = jnp.pad(places.astype(jnp.bfloat16)[None], ((0, NOTE - 1), (0, TS - count)))
    return jnp.concatenate([tiles.reshape(count * TS, TS), note])


def pack_left_kernel(place_ref, left_ref, right_zero, right_one, lefts, left_zero, rights):
    for column in range(HELD):
        targets = [part(lefts, column, BLOCK)] + [left_zero] * (column == 0)
        for target in targets:
            for q in range(SA):
                target[q * TS : (q + 1) * TS, :] = left_ref[column, q]
            write_note(target, place_ref, column, SA)
    rights[:PIECE, :] = right_zero[...]
    rights[PIECE:, :] = right_one[...]


def part(ref, column, rows):
    return ref.at[column * rows : (column + 1) * rows]


def mark_kernel(right_one, mark):
    mark[...] = jnp.zeros_like(mark)


def block_kernel(layer, mark, lefts, left_next, *refs, column):
    count = STEPS + column
    arriving, shares = list(refs[:count]), refs[count : count + TRIO]
    arriving[2] = part(arriving[2], column, PIECE)
    total, place_ref, pieces, last, sem = refs[count + TRIO :]
    targets = [pieces.at[step] for step in range(STEPS)] + [last] * column
    copies = [pltpu.make_async_copy(source, target, sem.at[n]) for n, (source, target) in enumerate(zip(arriving, targets))]
    for copy in copies:
        copy.start()
    blocks = [part(lefts, 0, BLOCK), part(lefts, 1, BLOCK), part(left_next, 0, BLOCK), part(left_next, 1, BLOCK), last]
    total[...] = jnp.zeros_like(total)
    for step in range(STEPS):
        copies[step].wait()
        if column and step == STEPS - 1:
            copies[STEPS].wait()
        add_term(total, place_ref, blocks[column + step], pieces.at[step])
    half = layer[0] // TRIO
    for turn, share in enumerate(shares):
        spot = lax.rem(layer[0] + turn, TRIO)
        for n, side in enumerate((half, 1 - half)):
            rows = pl.ds(pl.multiple_of((side * TRIO + spot) * SHARE, SHARE), SHARE)
            share[n * SHARE : (n + 1) * SHARE, :] = total[rows, :].astype(share.dtype)


def gather_kernel(own, one, two, near, far):
    added = own[...].astype(jnp.float32) + one[...].astype(jnp.float32) + two[...].astype(jnp.float32)
    near[...] = added[:SHARE]
    far[...] = added[SHARE:].astype(far.dtype)


def total_kernel(near, far, out_ref):
    out_ref[...] = (near[...] + far[...].astype(jnp.float32)).astype(out_ref.dtype)


def final_kernel(first, near, far, out_ref):
    out_ref[:, :TS] = first[...]
    total_kernel(near, far, out_ref.at[:, TS:])


AHEAD = 4 * 10**10
GATHER = 10**12
FIRST = 10**12
AFTER = 0
SMEM = pl.BlockSpec(memory_space=pltpu.SMEM)
VMEM = pl.BlockSpec(memory_space=pltpu.VMEM)
ANY = pl.BlockSpec(memory_space=pl.ANY)
PARAMS = pltpu.CompilerParams(vmem_limit_bytes=12 * 1024 * 1024)


def call(kernel, out_shape, in_specs, operands, scratch=(), cost=0):
    return pl.pallas_call(
        kernel,
        out_shape=out_shape,
        in_specs=in_specs,
        out_specs=jax.tree.map(lambda _: VMEM, out_shape),
        scratch_shapes=scratch,
        compiler_params=PARAMS,
        cost_estimate=pl.CostEstimate(flops=cost, bytes_accessed=0, transcendentals=0),
    )(*operands)


def array(rows, columns, dtype=jnp.bfloat16):
    return jax.ShapeDtypeStruct((rows, columns), dtype)


def body(left_tiles, left_place, right_tiles, right_place):
    layer = lax.axis_index("layer").astype(jnp.int32).reshape(1)
    right, right_at = right_tiles[0, 0], right_place[0, 0]
    pieces = [packed(right[j], right_at[j]) for j in range(HELD)]
    right_one = [shifted(piece, "row", -1) for piece in pieces]
    lefts, left_zero, rights = call(
        pack_left_kernel,
        [array(HELD * BLOCK, TS), array(BLOCK, TS), array(HELD * PIECE, TS)],
        [SMEM] + [VMEM] * 3,
        (left_place[0, 0], left_tiles[0, 0], *pieces),
    )
    right_two = shifted(rights, "row", -2)
    left_next = shifted(lefts, "col", -1)
    left_last = shifted(left_zero, "col", -2)
    mark = call(mark_kernel, array(8, 128, jnp.float32), [ANY], (right_one[1],), cost=AHEAD)
    right_two, left_next, mark = lax.optimization_barrier((right_two, left_next, mark))
    right_three = [shifted(piece, "row", -2) for piece in right_one]
    trio = [[(p, p // TRIO * TRIO + (p + turn) % TRIO) for p in range(2 * TRIO)] for turn in range(TRIO)]
    across = [(p, (p + TRIO) % (2 * TRIO)) for p in range(2 * TRIO)]
    shares = []
    for j in range(HELD):
        arriving = [pieces[j], right_one[j], right_two, right_three[j]] + [left_last] * j
        if j:
            arriving[0], shares[j - 1] = lax.optimization_barrier((arriving[0], shares[j - 1]))
        shares.append(
            call(
                functools.partial(block_kernel, column=j),
                [array(2 * SHARE, TS)] * TRIO,
                [SMEM, ANY] + [VMEM] * 2 + [ANY] * len(arriving),
                (layer, mark, lefts, left_next, *arriving),
                [
                    pltpu.VMEM((RT * TS, TS), jnp.float32),
                    pltpu.SMEM((3, SA), jnp.int32),
                    pltpu.VMEM((STEPS, PIECE, TS), jnp.bfloat16),
                    pltpu.VMEM((BLOCK, TS), jnp.bfloat16),
                    pltpu.SemaphoreType.DMA((STEPS + 1,)),
                ],
            )
        )
    ends = []
    for j, (own, *others) in enumerate(shares):
        arrived = [lax.ppermute(share, "layer", trio[turn]) for turn, share in enumerate(others, 1)]
        if j:
            arrived, ends = lax.optimization_barrier((arrived, ends))
        near, far = call(
            gather_kernel,
            [array(SHARE, TS, jnp.float32), array(SHARE, TS)],
            [VMEM] * TRIO,
            (own, *arrived),
            cost=(GATHER, AFTER)[j],
        )
        ends.append(near)
        shares[j] = lax.ppermute(far, "layer", across)
    first = call(total_kernel, array(SHARE, TS), [VMEM] * 2, (ends[0], shares[0]), cost=FIRST)
    return call(final_kernel, array(SHARE, HELD * TS), [VMEM] * 3, (first, ends[1], shares[1]))


def solution(mesh):
    return jax.shard_map(
        body,
        mesh=mesh,
        in_specs=(
            P("layer", "row", "col", None, None, None),
            P("layer", "row", "col", None),
            P("layer", "row", "col", None, None, None),
            P("layer", "row", "col", None),
        ),
        out_specs=P(("row", "layer"), "col"),
        check_vma=False,
    )
```

```python
import functools

import jax
import jax.numpy as jnp
from jax import lax
from jax.experimental import pallas as pl
from jax.experimental.pallas import tpu as pltpu
from jax.sharding import PartitionSpec as P

TS = 256
KT = 8
RT = 3
SA = 6
SB = 2
STEPS = 4
TRIO = 3
SHARE = 128
HELD = 2
NOTE = 16
PIECE = SB * TS + NOTE
BLOCK = SA * TS + NOTE


def shifted(block, axis, distance):
    size = lax.axis_size(axis)
    return lax.ppermute(block, axis, [((i - distance) % size, i) for i in range(size)])


def add_term(total, hit_ref, left_ref, right_ref):
    first, second = noted(right_ref, SB)
    left_places = noted(left_ref, SA)
    count = jnp.int32(0)
    for q in range(SA):
        place = left_places[q]
        inner = lax.rem(place, KT)
        hits_first = first == inner
        hit = (place >= 0) & (hits_first | (second == inner))

        @pl.when(hit)
        def _():
            hit_ref[0, count] = q * TS
            hit_ref[1, count] = jnp.where(hits_first, 0, TS)
            hit_ref[2, count] = (place // KT) * TS

        count = count + hit.astype(jnp.int32)

    def product(n, carry):
        left_rows, right_rows, rows = (pl.ds(pl.multiple_of(hit_ref[k, n], TS), TS) for k in range(3))
        total[rows, :] += jnp.dot(left_ref[left_rows, :], right_ref[right_rows, :], preferred_element_type=jnp.float32)
        return carry

    lax.fori_loop(0, count, product, 0)


def noted(packed_ref, slots):
    note = packed_ref[slots * TS : slots * TS + NOTE, :128].astype(jnp.float32).astype(jnp.int32)
    return [note[0, p] for p in range(slots)]


def write_note(packed_ref, place_ref, column, slots):
    shape = (NOTE, packed_ref.shape[1])
    lane = lax.broadcasted_iota(jnp.int32, shape, 1)
    note = jnp.full(shape, -1, jnp.int32)
    for p in range(slots):
        note = jnp.where(lane == p, place_ref[column, p], note)
    packed_ref[slots * TS :, :] = note.astype(jnp.float32).astype(jnp.bfloat16)


def packed(tiles, places):
    count = places.shape[0]
    note = jnp.pad(places.astype(jnp.bfloat16)[None], ((0, NOTE - 1), (0, TS - count)))
    return jnp.concatenate([tiles.reshape(count * TS, TS), note])


def pack_left_kernel(place_ref, left_ref, right_zero, right_one, lefts, left_zero, rights):
    for column in range(HELD):
        targets = [part(lefts, column, BLOCK)] + [left_zero] * (column == 0)
        for target in targets:
            for q in range(SA):
                target[q * TS : (q + 1) * TS, :] = left_ref[column, q]
            write_note(target, place_ref, column, SA)
    rights[:PIECE, :] = right_zero[...]
    rights[PIECE:, :] = right_one[...]


def part(ref, column, rows):
    return ref.at[column * rows : (column + 1) * rows]


def mark_kernel(right_one, mark):
    mark[...] = jnp.zeros_like(mark)


def block_kernel(layer, mark, lefts, left_next, *refs, column):
    count = STEPS + column
    arriving, shares = list(refs[:count]), refs[count : count + TRIO]
    arriving[2] = part(arriving[2], column, PIECE)
    total, place_ref, pieces, last, sem = refs[count + TRIO :]
    targets = [pieces.at[step] for step in range(STEPS)] + [last] * column
    copies = [pltpu.make_async_copy(source, target, sem.at[n]) for n, (source, target) in enumerate(zip(arriving, targets))]
    for copy in copies:
        copy.start()
    blocks = [part(lefts, 0, BLOCK), part(lefts, 1, BLOCK), part(left_next, 0, BLOCK), part(left_next, 1, BLOCK), last]
    total[...] = jnp.zeros_like(total)
    for step in range(STEPS):
        copies[step].wait()
        if column and step == STEPS - 1:
            copies[STEPS].wait()
        add_term(total, place_ref, blocks[column + step], pieces.at[step])
    half = layer[0] // TRIO
    for turn, share in enumerate(shares):
        spot = lax.rem(layer[0] + turn, TRIO)
        for n, side in enumerate((half, 1 - half)):
            rows = pl.ds(pl.multiple_of((side * TRIO + spot) * SHARE, SHARE), SHARE)
            share[n * SHARE : (n + 1) * SHARE, :] = total[rows, :].astype(share.dtype)


def gather_kernel(own, one, two, near, far):
    added = own[...].astype(jnp.float32) + one[...].astype(jnp.float32) + two[...].astype(jnp.float32)
    near[...] = added[:SHARE]
    far[...] = added[SHARE:].astype(far.dtype)


def total_kernel(near, far, out_ref):
    out_ref[...] = (near[...] + far[...].astype(jnp.float32)).astype(out_ref.dtype)


def final_kernel(first, near, far, out_ref):
    out_ref[:, :TS] = first[...]
    total_kernel(near, far, out_ref.at[:, TS:])


AHEAD = 2 * 10**10
GATHER = 3 * 10**9
FIRST = 3 * 10**9
AFTER = 0
SMEM = pl.BlockSpec(memory_space=pltpu.SMEM)
VMEM = pl.BlockSpec(memory_space=pltpu.VMEM)
ANY = pl.BlockSpec(memory_space=pl.ANY)
PARAMS = pltpu.CompilerParams(vmem_limit_bytes=12 * 1024 * 1024)


def call(kernel, out_shape, in_specs, operands, scratch=(), cost=0):
    return pl.pallas_call(
        kernel,
        out_shape=out_shape,
        in_specs=in_specs,
        out_specs=jax.tree.map(lambda _: VMEM, out_shape),
        scratch_shapes=scratch,
        compiler_params=PARAMS,
        cost_estimate=pl.CostEstimate(flops=cost, bytes_accessed=0, transcendentals=0),
    )(*operands)


def array(rows, columns, dtype=jnp.bfloat16):
    return jax.ShapeDtypeStruct((rows, columns), dtype)


def body(left_tiles, left_place, right_tiles, right_place):
    layer = lax.axis_index("layer").astype(jnp.int32).reshape(1)
    right, right_at = right_tiles[0, 0], right_place[0, 0]
    pieces = [packed(right[j], right_at[j]) for j in range(HELD)]
    right_one = [shifted(piece, "row", -1) for piece in pieces]
    lefts, left_zero, rights = call(
        pack_left_kernel,
        [array(HELD * BLOCK, TS), array(BLOCK, TS), array(HELD * PIECE, TS)],
        [SMEM] + [VMEM] * 3,
        (left_place[0, 0], left_tiles[0, 0], *pieces),
    )
    right_two = shifted(rights, "row", -2)
    left_next = shifted(lefts, "col", -1)
    left_last = shifted(left_zero, "col", -2)
    mark = call(mark_kernel, array(8, 128, jnp.float32), [ANY], (right_one[1],), cost=AHEAD)
    right_two, left_next, mark = lax.optimization_barrier((right_two, left_next, mark))
    right_three = [shifted(piece, "row", -2) for piece in right_one]
    trio = [[(p, p // TRIO * TRIO + (p + turn) % TRIO) for p in range(2 * TRIO)] for turn in range(TRIO)]
    across = [(p, (p + TRIO) % (2 * TRIO)) for p in range(2 * TRIO)]
    shares = []
    for j in range(HELD):
        arriving = [pieces[j], right_one[j], right_two, right_three[j]] + [left_last] * j
        if j:
            arriving[0], shares[j - 1] = lax.optimization_barrier((arriving[0], shares[j - 1]))
        shares.append(
            call(
                functools.partial(block_kernel, column=j),
                [array(2 * SHARE, TS)] * TRIO,
                [SMEM, ANY] + [VMEM] * 2 + [ANY] * len(arriving),
                (layer, mark, lefts, left_next, *arriving),
                [
                    pltpu.VMEM((RT * TS, TS), jnp.float32),
                    pltpu.SMEM((3, SA), jnp.int32),
                    pltpu.VMEM((STEPS, PIECE, TS), jnp.bfloat16),
                    pltpu.VMEM((BLOCK, TS), jnp.bfloat16),
                    pltpu.SemaphoreType.DMA((STEPS + 1,)),
                ],
            )
        )
    ends = []
    for j, (own, *others) in enumerate(shares):
        arrived = [lax.ppermute(share, "layer", trio[turn]) for turn, share in enumerate(others, 1)]
        if j:
            arrived, ends = lax.optimization_barrier((arrived, ends))
        near, far = call(
            gather_kernel,
            [array(SHARE, TS, jnp.float32), array(SHARE, TS)],
            [VMEM] * TRIO,
            (own, *arrived),
            cost=(GATHER, AFTER)[j],
        )
        ends.append(near)
        shares[j] = lax.ppermute(far, "layer", across)
    first = call(total_kernel, array(SHARE, TS), [VMEM] * 2, (ends[0], shares[0]), cost=FIRST)
    return call(final_kernel, array(SHARE, HELD * TS), [VMEM] * 3, (first, ends[1], shares[1]))


def solution(mesh):
    return jax.shard_map(
        body,
        mesh=mesh,
        in_specs=(
            P("layer", "row", "col", None, None, None),
            P("layer", "row", "col", None),
            P("layer", "row", "col", None, None, None),
            P("layer", "row", "col", None),
        ),
        out_specs=P(("row", "layer"), "col"),
        check_vma=False,
    )
```

```python
import functools

import jax
import jax.numpy as jnp
from jax import lax
from jax.experimental import pallas as pl
from jax.experimental.pallas import tpu as pltpu
from jax.sharding import PartitionSpec as P

TS = 256
KT = 8
RT = 3
SA = 6
SB = 2
STEPS = 4
TRIO = 3
SHARE = 128
HELD = 2
NOTE = 16
PIECE = SB * TS + NOTE
BLOCK = SA * TS + NOTE


def shifted(block, axis, distance):
    size = lax.axis_size(axis)
    return lax.ppermute(block, axis, [((i - distance) % size, i) for i in range(size)])


def add_term(total, hit_ref, left_ref, right_ref):
    first, second = noted(right_ref, SB)
    left_places = noted(left_ref, SA)
    count = jnp.int32(0)
    for q in range(SA):
        place = left_places[q]
        inner = lax.rem(place, KT)
        hits_first = first == inner
        hit = (place >= 0) & (hits_first | (second == inner))

        @pl.when(hit)
        def _():
            hit_ref[0, count] = q * TS
            hit_ref[1, count] = jnp.where(hits_first, 0, TS)
            hit_ref[2, count] = (place // KT) * TS

        count = count + hit.astype(jnp.int32)

    def product(n, carry):
        left_rows, right_rows, rows = (pl.ds(pl.multiple_of(hit_ref[k, n], TS), TS) for k in range(3))
        total[rows, :] += jnp.dot(left_ref[left_rows, :], right_ref[right_rows, :], preferred_element_type=jnp.float32)
        return carry

    lax.fori_loop(0, count, product, 0)


def noted(packed_ref, slots):
    note = packed_ref[slots * TS : slots * TS + NOTE, :128].astype(jnp.float32).astype(jnp.int32)
    return [note[0, p] for p in range(slots)]


def write_note(packed_ref, place_ref, column, slots):
    shape = (NOTE, packed_ref.shape[1])
    lane = lax.broadcasted_iota(jnp.int32, shape, 1)
    note = jnp.full(shape, -1, jnp.int32)
    for p in range(slots):
        note = jnp.where(lane == p, place_ref[column, p], note)
    packed_ref[slots * TS :, :] = note.astype(jnp.float32).astype(jnp.bfloat16)


def packed(tiles, places):
    count = places.shape[0]
    note = jnp.pad(places.astype(jnp.bfloat16)[None], ((0, NOTE - 1), (0, TS - count)))
    return jnp.concatenate([tiles.reshape(count * TS, TS), note])


def pack_left_kernel(place_ref, left_ref, right_zero, right_one, lefts, left_zero, rights):
    for column in range(HELD):
        targets = [part(lefts, column, BLOCK)] + [left_zero] * (column == 0)
        for target in targets:
            for q in range(SA):
                target[q * TS : (q + 1) * TS, :] = left_ref[column, q]
            write_note(target, place_ref, column, SA)
    rights[:PIECE, :] = right_zero[...]
    rights[PIECE:, :] = right_one[...]


def part(ref, column, rows):
    return ref.at[column * rows : (column + 1) * rows]


def mark_kernel(right_one, mark):
    mark[...] = jnp.zeros_like(mark)


def block_kernel(layer, mark, lefts, left_next, *refs, column):
    count = STEPS + column
    arriving, shares = list(refs[:count]), refs[count : count + TRIO]
    arriving[2] = part(arriving[2], column, PIECE)
    total, place_ref, pieces, last, sem = refs[count + TRIO :]
    targets = [pieces.at[step] for step in range(STEPS)] + [last] * column
    copies = [pltpu.make_async_copy(source, target, sem.at[n]) for n, (source, target) in enumerate(zip(arriving, targets))]
    for n in (0, 1, 3, 2, *range(STEPS, count)):
        copies[n].start()
    blocks = [part(lefts, 0, BLOCK), part(lefts, 1, BLOCK), part(left_next, 0, BLOCK), part(left_next, 1, BLOCK), last]
    total[...] = jnp.zeros_like(total)
    for step in range(STEPS):
        copies[step].wait()
        if column and step == STEPS - 1:
            copies[STEPS].wait()
        add_term(total, place_ref, blocks[column + step], pieces.at[step])
    half = layer[0] // TRIO
    for turn, share in enumerate(shares):
        spot = lax.rem(layer[0] + turn, TRIO)
        for n, side in enumerate((half, 1 - half)):
            rows = pl.ds(pl.multiple_of((side * TRIO + spot) * SHARE, SHARE), SHARE)
            share[n * SHARE : (n + 1) * SHARE, :] = total[rows, :].astype(share.dtype)


def gather_kernel(own, one, two, near, far):
    added = own[...].astype(jnp.float32) + one[...].astype(jnp.float32) + two[...].astype(jnp.float32)
    near[...] = added[:SHARE]
    far[...] = added[SHARE:].astype(far.dtype)


def total_kernel(near, far, out_ref):
    out_ref[...] = (near[...] + far[...].astype(jnp.float32)).astype(out_ref.dtype)


def final_kernel(first, near, far, out_ref):
    out_ref[:, :TS] = first[...]
    total_kernel(near, far, out_ref.at[:, TS:])


AHEAD = 2 * 10**10
GATHER = 3 * 10**9
FIRST = 3 * 10**9
AFTER = 0
SMEM = pl.BlockSpec(memory_space=pltpu.SMEM)
VMEM = pl.BlockSpec(memory_space=pltpu.VMEM)
ANY = pl.BlockSpec(memory_space=pl.ANY)
PARAMS = pltpu.CompilerParams(vmem_limit_bytes=12 * 1024 * 1024)


def call(kernel, out_shape, in_specs, operands, scratch=(), cost=0):
    return pl.pallas_call(
        kernel,
        out_shape=out_shape,
        in_specs=in_specs,
        out_specs=jax.tree.map(lambda _: VMEM, out_shape),
        scratch_shapes=scratch,
        compiler_params=PARAMS,
        cost_estimate=pl.CostEstimate(flops=cost, bytes_accessed=0, transcendentals=0),
    )(*operands)


def array(rows, columns, dtype=jnp.bfloat16):
    return jax.ShapeDtypeStruct((rows, columns), dtype)


def body(left_tiles, left_place, right_tiles, right_place):
    layer = lax.axis_index("layer").astype(jnp.int32).reshape(1)
    right, right_at = right_tiles[0, 0], right_place[0, 0]
    pieces = [packed(right[j], right_at[j]) for j in range(HELD)]
    right_one = [shifted(piece, "row", -1) for piece in pieces]
    lefts, left_zero, rights = call(
        pack_left_kernel,
        [array(HELD * BLOCK, TS), array(BLOCK, TS), array(HELD * PIECE, TS)],
        [SMEM] + [VMEM] * 3,
        (left_place[0, 0], left_tiles[0, 0], *pieces),
    )
    right_two = shifted(rights, "row", -2)
    left_next = shifted(lefts, "col", -1)
    left_last = shifted(left_zero, "col", -2)
    mark = call(mark_kernel, array(8, 128, jnp.float32), [ANY], (right_one[1],), cost=AHEAD)
    right_two, left_next, mark = lax.optimization_barrier((right_two, left_next, mark))
    right_three = [shifted(piece, "row", -2) for piece in right_one]
    trio = [[(p, p // TRIO * TRIO + (p + turn) % TRIO) for p in range(2 * TRIO)] for turn in range(TRIO)]
    across = [(p, (p + TRIO) % (2 * TRIO)) for p in range(2 * TRIO)]
    shares = []
    for j in range(HELD):
        arriving = [pieces[j], right_one[j], right_two, right_three[j]] + [left_last] * j
        if j:
            arriving[0], shares[j - 1] = lax.optimization_barrier((arriving[0], shares[j - 1]))
        shares.append(
            call(
                functools.partial(block_kernel, column=j),
                [array(2 * SHARE, TS)] * TRIO,
                [SMEM, ANY] + [VMEM] * 2 + [ANY] * len(arriving),
                (layer, mark, lefts, left_next, *arriving),
                [
                    pltpu.VMEM((RT * TS, TS), jnp.float32),
                    pltpu.SMEM((3, SA), jnp.int32),
                    pltpu.VMEM((STEPS, PIECE, TS), jnp.bfloat16),
                    pltpu.VMEM((BLOCK, TS), jnp.bfloat16),
                    pltpu.SemaphoreType.DMA((STEPS + 1,)),
                ],
            )
        )
    ends = []
    for j, (own, *others) in enumerate(shares):
        arrived = [lax.ppermute(share, "layer", trio[turn]) for turn, share in enumerate(others, 1)]
        if j:
            arrived, ends = lax.optimization_barrier((arrived, ends))
        near, far = call(
            gather_kernel,
            [array(SHARE, TS, jnp.float32), array(SHARE, TS)],
            [VMEM] * TRIO,
            (own, *arrived),
            cost=(GATHER, AFTER)[j],
        )
        ends.append(near)
        shares[j] = lax.ppermute(far, "layer", across)
    first = call(total_kernel, array(SHARE, TS), [VMEM] * 2, (ends[0], shares[0]), cost=FIRST)
    return call(final_kernel, array(SHARE, HELD * TS), [VMEM] * 3, (first, ends[1], shares[1]))


def solution(mesh):
    return jax.shard_map(
        body,
        mesh=mesh,
        in_specs=(
            P("layer", "row", "col", None, None, None),
            P("layer", "row", "col", None),
            P("layer", "row", "col", None, None, None),
            P("layer", "row", "col", None),
        ),
        out_specs=P(("row", "layer"), "col"),
        check_vma=False,
    )
```
